512 devices in a mesh: wide: 64 (over y, x, core), narrow: 8 (over z).
Axes of the slice: x: 4, y: 8, z: 8, core: 2. Of those that a mesh axis runs over, the one named last changes fastest.
Arguments:
- amplitudes: bfloat16 [256, 128, 4096], P('wide', None, 'narrow'), may hold values from -6 to 6
- int_values: bfloat16 [192, 4096], P('narrow'), may hold values from -0.5 to 0.5
- hole_ladder: bfloat16 [256, 256], replicated, may hold values from -0.375 to 0.375
- amp_tiles: int32 [128], replicated, may hold values from 0 to 575, as said below
- int_tiles: int32 [192], replicated, may hold values from 0 to 575, as said below
- owner: int32 [128, 1], replicated, may hold values from 0 to 63; in each aligned block of 128 rows (0 to 127, 128 to 255, ...) at most 4 rows name the same one
Outputs:
- residual: bfloat16 [256, 256, 4096], P(None, 'wide', 'narrow')
The draws below stay inside these ranges and needn't reach their ends.
Inputs may be any that keep to these rules, and one draw needn't show every extreme that they name: `amp_tiles`: 128 distinct codes, each first tile * 24 + second tile; no first tile has more than 6 codes, and some first tile has exactly 6. `int_tiles`: 192 distinct codes, each first tile * 24 + second tile; codes 0 and 575 are always among them. `owner`: every index of wide owns at least one and at most 4 amplitude tiles; some index owns exactly 4.
All inputs are finite; a program needn't handle non-finite values.
Results may differ from the reference program's by a relative error of at most 0.0038.
Values may be sent and summed in bfloat16 or wider, within the bound.
A program may use at most 128 MiB of HBM per device.

```python
import math
import jax
import jax.numpy as jnp
import numpy as np
from jax import lax

TILE = 64
NVT = 24
KI = 192
KT = 128
CAP = 4
PAIRS = 256
SLOTS = 256
N_WIDE = 64


def pick_codes(key, list_length):
    first_key, second_key = jax.random.split(key)
    span = NVT * NVT
    interior = 1 + jax.random.permutation(first_key, span - 2)[:list_length - 2]
    tile_codes = jnp.concatenate([jnp.array([0, span - 1], dtype=jnp.int32), interior.astype(jnp.int32)])
    return jax.random.permutation(second_key, tile_codes).astype(jnp.int32)


def draw_amp_tiles(key, part):
    key = jax.random.fold_in(key, 11)
    count_key, column_key, order_key = jax.random.split(key, 3)
    base_count = KT // NVT
    extra_rows = KT % NVT
    row_most = (KT + NVT - 1) // NVT
    row_rank = jax.random.permutation(count_key, NVT)
    row_counts = base_count + (row_rank < extra_rows).astype(jnp.int32)
    column_keys = jax.random.split(column_key, NVT)
    columns = jax.vmap(lambda one_key: jax.random.permutation(one_key, NVT))(column_keys)[:, :row_most]
    row_ids = jnp.arange(NVT, dtype=jnp.int32)[:, None]
    all_codes = (row_ids * NVT + columns.astype(jnp.int32)).reshape(-1)
    valid = (jnp.arange(row_most, dtype=jnp.int32)[None, :] < row_counts[:, None]).reshape(-1)
    order = jnp.argsort(jnp.where(valid, 0, 1).astype(jnp.int32), stable=True)[:KT]
    chosen = all_codes[order].astype(jnp.int32)
    return jax.random.permutation(order_key, chosen).astype(jnp.int32)


def draw_int_tiles(key, part):
    key = jax.random.fold_in(key, 23)
    return pick_codes(key, KI)


def steps_of(own_key, shape, cuts, least, high):
    def one(dim, shards_of):
        draws = jax.random.uniform(jax.random.fold_in(jax.random.fold_in(own_key, 6), dim), (shards_of,), jnp.float32, least / len(cuts), high / len(cuts))
        return jnp.repeat(jnp.exp(draws), shape[dim] // shards_of).reshape((-1,) + (1,) * (len(shape) - dim - 1))

    factor_of = one(*cuts[0])
    for cut in cuts[1:]:
        factor_of = factor_of * one(*cut)
    return factor_of


def deal_out(own_key, own, number, rows, number_of, top, most, skew):
    sequence = jax.random.permutation(own_key, number_of)
    crowded, common = portions_of(number_of, rows * top, most, skew, True), portions_of(number_of, rows * top, most, skew, False)
    places = jnp.arange(number_of)

    def named(sizes, turn):
        used = int((sizes > 0).sum())
        fixed = max(1, used // 4)
        shifted = fixed + (places - fixed + turn * (used - fixed)) % max(1, number_of - fixed)
        return jnp.zeros((number_of,), jnp.int32).at[sequence[jnp.where(places < fixed, places, shifted)]].set(jnp.asarray(sizes, jnp.int32))

    sizes = jnp.where(number % 4 == 0, named(crowded, number // 4), named(common, number - number // 4 - 1))
    mixed = jax.random.permutation(jax.random.fold_in(own, 3), number_of)
    giver, sink = mixed[0:number_of // 2 * 2:2], mixed[1:number_of // 2 * 2:2]
    slack = jnp.minimum(sizes[giver] - 1, most - sizes[sink]) // 2
    slack = jnp.where((giver == sequence[0]) | (sink == sequence[0]) | (sizes[sink] == 0), 0, jnp.maximum(slack, 0))
    shifted = jax.random.randint(jax.random.fold_in(own, 4), (number_of // 2,), 0, 1 << 20) % (slack + 1)
    sizes = sizes.at[giver].add(-shifted).at[sink].add(shifted)
    items = jnp.searchsorted(jnp.cumsum(sizes), jnp.arange(rows * top), side="right").astype(jnp.int32)
    listing = items.reshape(top, rows).T
    listing = listing[jax.random.permutation(jax.random.fold_in(own, 1), rows)]
    turn = jax.random.randint(jax.random.fold_in(own, 2), (rows, 1), 0, top)
    return jnp.take_along_axis(listing, (jnp.arange(top)[None, :] + turn) % top, axis=1)


def portions_of(amount, total, most, lean, full):
    loads = [(1 << 20) // math.isqrt(grade ** lean) + 1 for grade in range(1, amount + 1)]
    largest = most if full else min(most, max(-(-total // amount), total * loads[0] // sum(loads)))
    least = 1 if total - largest >= amount - 1 else 0
    holding, surplus = [largest] + [least] * (amount - 1), total - largest - least * (amount - 1)
    while surplus > 0:
        free = [i for i in range(1, amount) if holding[i] < largest] or [i for i in range(1, amount) if holding[i] < most]
        pool, budget = sum([loads[i] for i in free]), surplus
        for i in free:
            more = min(most - holding[i], max(1, budget * loads[i] // pool), surplus)
            holding[i] = holding[i] + more
            surplus = surplus - more
    return np.array(holding)


def noise(rng, dims, scale, limit, pieces=(), held_as=jnp.bfloat16):
    values = scale * jax.random.normal(rng, dims, jnp.float32)
    if pieces:
        values = values * steps_of(rng, dims, pieces, -0.22, 0.18)
    return jnp.clip(values, -limit, limit).astype(held_as)


def setup_inputs(seed: int = 0) -> dict:
    splits = jax.random.split(jax.random.key(seed), 7)
    amplitudes = noise(splits[0], (PAIRS, KT, TILE * TILE), 1.0, 6.0, ((0, 64), (2, 8)))
    int_values = noise(splits[1], (KI, TILE * TILE), (2 * TILE) ** -0.5, 0.5, ((0, 8),))
    hole_ladder = noise(splits[2], (PAIRS, PAIRS), PAIRS ** -0.5, 0.375)
    amp_tiles = draw_amp_tiles(jax.random.fold_in(splits[6], 71), 0)
    int_tiles = draw_int_tiles(jax.random.fold_in(splits[6], 71), 0)
    owner_keys = jax.random.split(jax.random.fold_in(splits[5], 1), KT // KT)
    owner_turns = jax.random.permutation(jax.random.fold_in(splits[5], 3), KT // KT)
    owner = jax.vmap(lambda own, number: deal_out(jax.random.fold_in(splits[5], 2), own, number, KT, N_WIDE, 1, CAP, 2))(owner_keys, owner_turns).reshape((KT, 1))
    return {"amplitudes": amplitudes, "int_values": int_values, "hole_ladder": hole_ladder, "amp_tiles": amp_tiles, "int_tiles": int_tiles, "owner": owner}


def tile_table(tile_codes, list_length):
    codes_grid = jnp.arange(NVT * NVT, dtype=jnp.int32)
    matches = codes_grid[:, None] == tile_codes[None, :]
    number = jnp.arange(list_length, dtype=jnp.int32)
    located = jnp.sum(jnp.where(matches, number[None, :], 0), axis=1).astype(jnp.int32)
    present = jnp.any(matches, axis=1)
    return jnp.where(present, located, list_length).astype(jnp.int32).reshape(NVT, NVT)


def slot_table(owner, list_length, slot_count):
    owners = owner[:, 0].astype(jnp.int32)
    number = jnp.arange(list_length, dtype=jnp.int32)
    earlier = (owners[:, None] == owners[None, :]) & (number[None, :] < number[:, None])
    earlier_count = jnp.sum(earlier.astype(jnp.int32), axis=1).astype(jnp.int32)
    position = owners * CAP + earlier_count
    slot_ids = jnp.arange(slot_count, dtype=jnp.int32)
    matches = slot_ids[:, None] == position[None, :]
    located = jnp.sum(jnp.where(matches, number[None, :], 0), axis=1).astype(jnp.int32)
    return jnp.where(jnp.any(matches, axis=1), located, list_length).astype(jnp.int32)


def reference(amplitudes, int_values, hole_ladder, amp_tiles, int_tiles, owner):
    amp_table = tile_table(amp_tiles, KT)
    int_table = tile_table(int_tiles, KI)
    row_tile = amp_tiles // NVT
    col_tile = amp_tiles % NVT
    amp_pad = jnp.concatenate([amplitudes, jnp.zeros((PAIRS, 1, TILE * TILE), amplitudes.dtype)], axis=1)
    int_pad = jnp.concatenate([int_values, jnp.zeros((1, TILE * TILE), int_values.dtype)], axis=0)

    def one_tile(tile_index):
        amp_ids = amp_table[row_tile[tile_index]]
        int_ids = int_table[col_tile[tile_index]]
        left_tiles = amp_pad[:, amp_ids].astype(jnp.float32).reshape(PAIRS, NVT, TILE, TILE)
        right_tiles = int_pad[int_ids].astype(jnp.float32).reshape(NVT, TILE, TILE)
        dressed = jnp.einsum("pvad,vbd->pab", left_tiles, right_tiles).reshape(PAIRS, TILE * TILE)
        dressed = lax.optimization_barrier(dressed.astype(jnp.bfloat16))
        column = lax.dynamic_index_in_dim(amplitudes, tile_index, 1, keepdims=False)
        ladder = jnp.dot(hole_ladder, column, preferred_element_type=jnp.float32)
        return (ladder + dressed.astype(jnp.float32)).astype(jnp.bfloat16)

    tile_sum = lax.map(one_tile, jnp.arange(KT, dtype=jnp.int32))
    padded = jnp.concatenate([tile_sum, jnp.zeros((1, PAIRS, TILE * TILE), tile_sum.dtype)], axis=0)
    placed = padded[slot_table(owner, KT, SLOTS)]
    return jnp.transpose(placed, (1, 0, 2))
```

```python
import functools

import jax
import jax.numpy as jnp
from jax import lax
from jax.experimental import pallas as pl
from jax.experimental.pallas import tpu as pltpu
from jax.sharding import PartitionSpec as P

TILE = 64
NVT = 24
CAP = 4
MESH = pl.DeviceIdType.MESH
NT = (((1,), (1,)), ((), ()))
BF16, F32, I32 = jnp.bfloat16, jnp.float32, jnp.int32


def iota(shape, dim):
    return lax.broadcasted_iota(I32, shape, dim)


def hot(mask):
    return jnp.where(mask, 1.0, 0.0).astype(BF16)


def mm(a, b):
    return jnp.dot(a, b, preferred_element_type=F32)


def column_of(row):
    n = row.shape[1]
    eye = iota((n, n), 0) == iota((n, n), 1)
    return jnp.sum(jnp.where(eye, row, 0), axis=1, keepdims=True)


def kernel(wn, zn, table_ref, amp_ref, int_ref, hole_ref, codes_ref, owner_ref, out_ref,
           gath, tiles, idense, adense, zbuf, dress, pick, send_a, send_d, recv_a, recv_d, hexp, acc,
           z_send, z_recv, c_send, c_recv, a_send, a_recv, d_send, d_recv):
    wide = lax.axis_index("wide")
    narrow = lax.axis_index("narrow")
    core = lax.rem(wide, 2)
    other = wide + 1 - 2 * core
    cells = amp_ref.shape[1]
    blocks = cells // 128
    pairs = hole_ref.shape[0] // wn
    kt = amp_ref.shape[0] // pairs
    rows = CAP * pairs
    ki = tiles.shape[0] - 1
    share = ki // zn
    half_rows = share * 16
    cells_all = NVT * NVT
    low = iota((1, 128), 1) < TILE

    barrier = pltpu.get_barrier_semaphore()
    ring = sorted({1, zn - 1})

    def greet(i, c):
        pl.semaphore_signal(barrier, inc=1, device_id=(lax.rem(wide + i, wn), narrow), device_id_type=MESH)
        return c

    for step in ring:
        pl.semaphore_signal(barrier, inc=1, device_id=(wide, lax.rem(narrow + step, zn)), device_id_type=MESH)
    lax.fori_loop(1, wn, greet, 0)

    owner_row = owner_ref[...]
    owner_col = column_of(owner_row)
    before = iota((kt, kt), 0) < iota((kt, kt), 1)
    count = jnp.sum(jnp.where(before & (owner_col == owner_row), 1, 0), axis=0, keepdims=True)
    place = (owner_row * CAP + count) * pairs
    place = jnp.concatenate([place + p for p in range(pairs)], axis=1)
    pick[...] = hot(iota((wn * rows, pairs * kt), 0) == place)

    pl.semaphore_wait(barrier, wn - 1 + len(ring))

    right_hops, left_hops = zn // 2, (zn - 1) // 2

    def half(ref, shard, who):
        return ref.at[shard, pl.ds(pl.multiple_of(who * half_rows, 16), half_rows)]

    def hop(way, step, do):
        sign = 1 if way == 0 else zn - 1
        shard = lax.rem(narrow + (zn - sign) * (step - 1), zn)
        src = half(gath, shard, core) if step > 1 else int_ref.at[
            pl.ds(pl.multiple_of(core * half_rows, 16), half_rows)]
        k = step - 1 if way == 0 else right_hops + step - 1
        copy = pltpu.make_async_remote_copy(
            src_ref=src, dst_ref=half(gath, shard, core), send_sem=z_send.at[k], recv_sem=z_recv.at[k],
            device_id=(wide, lax.rem(narrow + sign, zn)), device_id_type=MESH)
        do(copy)

    def hand(way, step, do):
        sign = 1 if way == 0 else zn - 1
        shard = lax.rem(narrow + (zn - sign) * step, zn)
        k = step - 1 if way == 0 else right_hops + step - 1
        copy = pltpu.make_async_remote_copy(
            src_ref=half(gath, shard, core), dst_ref=half(gath, shard, core), send_sem=c_send.at[k],
            recv_sem=c_recv.at[k], device_id=(other, narrow), device_id_type=MESH)
        do(copy)

    def spread(block, first):
        n = block.shape[0] // 32
        x = block.astype(F32)
        y = pltpu.roll(x, TILE, 1)
        even = jnp.where(low, x, y).astype(BF16).reshape(n, 32, 128)
        odd = jnp.where(low, y, x).astype(BF16).reshape(n, 32, 128)
        tiles[pl.ds(first, n), pl.ds(0, 32)] = even
        tiles[pl.ds(first, n), pl.ds(32, 32)] = odd

    def spread_half(way, step, who):
        sign = 1 if way == 0 else zn - 1
        shard = lax.rem(narrow + (zn - sign) * step, zn)
        spread(half(gath, shard, who)[...], shard * share + who * (share // 2))

    hops = [(w, s) for s in range(1, right_hops + 1) for w in (0, 1) if s <= (right_hops, left_hops)[w]]
    start = lambda copy: copy.start()
    for w, s in hops:
        if s == 1:
            hop(w, s, start)

    def post(send, recv, s_sem, r_sem, do):
        def one(i, c):
            i = lax.rem(i + 3 * wn // 8, wn - 1) + 1
            to = lax.rem(wide + i, wn)
            copy = pltpu.make_async_remote_copy(
                src_ref=send.at[pl.ds(pl.multiple_of(to * rows, 16), rows)],
                dst_ref=recv.at[pl.ds(pl.multiple_of(wide * rows, 16), rows)],
                send_sem=s_sem.at[i], recv_sem=r_sem.at[i], device_id=(to, narrow), device_id_type=MESH)
            do(copy)
            return c
        lax.fori_loop(0, wn - 1, one, 0)

    send_a[...] = mm(pick[...], amp_ref[...]).astype(BF16)
    post(send_a, recv_a, a_send, a_recv, start)
    mine = pl.ds(pl.multiple_of(wide * rows, 16), rows)
    recv_a[mine] = send_a[mine]

    tiles[ki] = jnp.zeros((TILE, 128), BF16)
    spread(int_ref[...], narrow * share)

    codes = codes_ref[...]
    second = lax.rem(codes, NVT)
    cell = lax.rem(second, 2) * (cells_all // 2) + lax.div(second, 2) * NVT + lax.div(codes, NVT)
    onto = hot(iota((cells_all, kt), 0) == cell)

    def dense_pair(p):
        g = mm(onto, amp_ref[pl.ds(p * kt, kt), :])
        hf = cells_all // 2
        for m in range(blocks):
            ge, go = g[:hf, m * 128:(m + 1) * 128], g[hf:, m * 128:(m + 1) * 128]
            y0 = jnp.where(low, ge, pltpu.roll(go, TILE, 1))
            y1 = jnp.where(low, pltpu.roll(ge, TILE, 1), go)
            for h in range(NVT // 2):
                both = jnp.concatenate([y0[h * NVT:(h + 1) * NVT], y1[h * NVT:(h + 1) * NVT]], axis=0)
                adense[pl.ds((p * blocks + m) * 2 * NVT, 2 * NVT), pl.ds(h * 128, 128)] = both.astype(BF16)

    rounds = [[(w, s) for w, s in hops if s == r] for r in range(1, right_hops + 1)]
    todo = list(range(pairs))
    for r, ready in enumerate(rounds):
        if todo:
            dense_pair(todo.pop(0))
        for w, s in ready:
            hop(w, s, lambda copy: copy.wait_recv())
            hand(w, s, start)
            if (w, s + 1) in hops:
                hop(w, s + 1, start)
        for w, s in ready:
            spread_half(w, s, core)
    for p in todo:
        dense_pair(p)
    for w, s in hops:
        hand(w, s, lambda copy: copy.wait_recv())
        spread_half(w, s, 1 - core)

    def gather_row(c, carry):
        for h in range(NVT // 2):
            left = tiles[table_ref[c * NVT + 2 * h]]
            right = tiles[table_ref[c * NVT + 2 * h + 1]]
            idense[pl.ds(pl.multiple_of(c * TILE, TILE), TILE), pl.ds(h * 128, 128)] = jnp.where(low, left, right)
        return carry

    lax.fori_loop(0, NVT, gather_row, 0)

    def product(n, carry):
        rhs = idense[pl.ds(pl.multiple_of(n * 256, 256), 256), :]
        d = lax.dot_general(adense[...], rhs, NT, preferred_element_type=F32)
        for p in range(pairs):
            for m in range(blocks):
                at = (p * blocks + m) * 2 * NVT
                z0, z1 = [], []
                for j in range(2):
                    x0 = d[at:at + NVT, j * 128:(j + 1) * 128]
                    x1 = d[at + NVT:at + 2 * NVT, j * 128:(j + 1) * 128]
                    z0.append(jnp.where(low, x0, pltpu.roll(x1, TILE, 1)))
                    z1.append(jnp.where(low, pltpu.roll(x0, TILE, 1), x1))
                to = pl.multiple_of(n * 2 * NVT, 16)
                zbuf[p, pl.ds(to, 2 * NVT), pl.ds(m * 128, 128)] = jnp.concatenate(z0, axis=0).astype(BF16)
                zbuf[p, pl.ds(to + cells_all // 2, 2 * NVT), pl.ds(m * 128, 128)] = jnp.concatenate(
                    z1, axis=0).astype(BF16)
        return carry

    lax.fori_loop(0, NVT // 4, product, 0)

    off = iota((kt, cells_all), 1) == column_of(cell)
    take = hot(off)
    u, v = iota((128, 128), 0), iota((128, 128), 1)
    back = hot(v == (u & 64) + (u & 31) * 2 + ((u >> 5) & 1))
    for p in range(pairs):
        got = mm(take, zbuf[p]).astype(BF16)
        for m in range(blocks):
            dress[pl.ds(p * kt, kt), pl.ds(m * 128, 128)] = mm(got[:, m * 128:(m + 1) * 128], back).astype(BF16)
    send_d[...] = mm(pick[...], dress[...]).astype(BF16)
    post(send_d, recv_d, d_send, d_recv, start)
    recv_d[mine] = send_d[mine]

    total = wn * rows
    np_all = hole_ref.shape[0]
    r0, c0 = iota((total, np_all), 0), iota((total, np_all), 1)
    by_row = mm(hot(lax.div(r0, CAP) == c0), hole_ref[...]).astype(BF16)
    r1, c1 = iota((np_all, total), 0), iota((np_all, total), 1)
    spread_cols = hot(lax.div(c1, rows) * pairs + lax.rem(c1, pairs) == r1)
    chunk = 8 * rows if wn % 8 == 0 else total
    r2, c2 = iota((chunk, total), 0), iota((chunk, total), 1)
    same = lax.rem(r2, CAP) == lax.rem(lax.div(c2, pairs), CAP)
    for y in range(total // chunk):
        hexp[pl.ds(y * chunk, chunk), :] = jnp.where(
            same, mm(by_row[y * chunk:(y + 1) * chunk], spread_cols), 0.0).astype(BF16)

    post(send_a, recv_a, a_send, a_recv, lambda copy: copy.wait_recv())

    def ladder(y, carry):
        at = pl.ds(pl.multiple_of(y * chunk, 16), chunk)
        acc[at, :] = mm(hexp[at, :], recv_a[...])
        return carry

    lax.fori_loop(0, total // chunk, ladder, 0)

    post(send_d, recv_d, d_send, d_recv, lambda copy: copy.wait_recv())
    r3, c3 = iota((chunk, chunk), 0), iota((chunk, chunk), 1)
    want = lax.div(r3, rows) * rows + lax.rem(r3, CAP) * pairs + lax.rem(lax.div(r3, CAP), pairs)
    turn = hot(c3 == want)

    def finish(y, carry):
        at = pl.ds(pl.multiple_of(y * chunk, 16), chunk)
        out_ref[at, :] = (acc[at, :] + mm(turn, recv_d[at, :])).astype(BF16)
        return carry

    lax.fori_loop(0, total // chunk, finish, 0)

    for w, s in hops:
        hop(w, s, lambda copy: copy.wait_send())
        hand(w, s, lambda copy: copy.wait_send())
    post(send_a, recv_a, a_send, a_recv, lambda copy: copy.wait_send())
    post(send_d, recv_d, d_send, d_recv, lambda copy: copy.wait_send())


def per_device(wn, zn, amplitudes, int_values, hole_ladder, amp_tiles, int_tiles, owner):
    pairs, kt, cells = amplitudes.shape
    share = int_values.shape[0]
    ki = share * zn
    rows = CAP * pairs
    total = wn * rows
    blocks = cells // 128
    matches = jnp.arange(NVT * NVT, dtype=I32)[:, None] == int_tiles[None, :]
    table = ki + jnp.sum(jnp.where(matches, jnp.arange(ki, dtype=I32)[None, :] - ki, 0), axis=1)
    hops = zn - 1
    vmem = pl.BlockSpec(memory_space=pltpu.VMEM)
    out = pl.pallas_call(
        functools.partial(kernel, wn, zn),
        out_shape=jax.ShapeDtypeStruct((total, cells), BF16),
        in_specs=[pl.BlockSpec(memory_space=pltpu.SMEM)] + [vmem] * 5,
        out_specs=vmem,
        scratch_shapes=[
            pltpu.VMEM((zn, share * 32, 128), BF16),
            pltpu.VMEM((ki + 1, TILE, 128), BF16),
            pltpu.VMEM((NVT * TILE, NVT * TILE), BF16),
            pltpu.VMEM((pairs * blocks * 2 * NVT, NVT * TILE), BF16),
            pltpu.VMEM((pairs, NVT * NVT, cells), BF16),
            pltpu.VMEM((pairs * kt, cells), BF16),
            pltpu.VMEM((total, pairs * kt), BF16),
            pltpu.VMEM((total, cells), BF16),
            pltpu.VMEM((total, cells), BF16),
            pltpu.VMEM((total, cells), BF16),
            pltpu.VMEM((total, cells), BF16),
            pltpu.VMEM((total, total), BF16),
            pltpu.VMEM((total, cells), F32),
            pltpu.SemaphoreType.DMA((hops,)),
            pltpu.SemaphoreType.DMA((hops,)),
            pltpu.SemaphoreType.DMA((hops,)),
            pltpu.SemaphoreType.DMA((hops,)),
            pltpu.SemaphoreType.DMA((wn,)),
            pltpu.SemaphoreType.DMA((wn,)),
            pltpu.SemaphoreType.DMA((wn,)),
            pltpu.SemaphoreType.DMA((wn,)),
        ],
        compiler_params=pltpu.CompilerParams(
            collective_id=0, has_side_effects=True, vmem_limit_bytes=58 * 1024 * 1024
        ),
        cost_estimate=pl.CostEstimate(flops=8 * 10**9, bytes_accessed=4 * 10**6, transcendentals=0),
    )(
        table,
        amplitudes.reshape(pairs * kt, cells),
        int_values.reshape(share * 32, 128),
        hole_ladder,
        amp_tiles.reshape(1, kt),
        owner.reshape(1, kt),
    )
    return out.reshape(wn * pairs, CAP, cells)


def solution(mesh):
    wn, zn = mesh.shape["wide"], mesh.shape["narrow"]
    return jax.shard_map(
        functools.partial(per_device, wn, zn),
        mesh=mesh,
        in_specs=(P("wide", None, "narrow"), P("narrow", None), P(), P(), P(), P()),
        out_specs=P(None, "wide", "narrow"),
        check_vma=False,
    )
```

```python
import functools

import jax
import jax.numpy as jnp
from jax import lax
from jax.experimental import pallas as pl
from jax.experimental.pallas import tpu as pltpu
from jax.sharding import PartitionSpec as P

TILE = 64
NVT = 24
CAP = 4
ROW = 8
ROOMS = (20, 24, 32)
MESH = pl.DeviceIdType.MESH
NT = (((1,), (1,)), ((), ()))
BF16, F32, I32 = jnp.bfloat16, jnp.float32, jnp.int32


def iota(shape, dim):
    return lax.broadcasted_iota(I32, shape, dim)


def hot(mask):
    return jnp.where(mask, 1.0, 0.0).astype(BF16)


def mm(a, b):
    return jnp.dot(a, b, preferred_element_type=F32)


def column_of(row):
    n = row.shape[1]
    eye = iota((n, n), 0) == iota((n, n), 1)
    return jnp.sum(jnp.where(eye, row, 0), axis=1, keepdims=True)


def far_first(n):
    return sorted(range(1, n), key=lambda d: (-min(d, n - d), d))


def begin(copy):
    copy.start()


def landed(copy):
    copy.wait_recv()


def left(copy):
    copy.wait_send()


def kernel(wn, zn, room, table_ref, amp_ref, int_ref, hole_ref, codes_ref, owner_ref, out_ref,
           local, local32, gath, tiles, idense, adense, zbuf, dress, pick, pack_a, pack_d, leg_a, leg_d,
           turn_a, turn_d, recv_a, recv_d, hexp, acc,
           z_send, z_recv, x_send, x_recv, c_send, c_recv,
           ya_send, ya_recv, yd_send, yd_recv, ra_send, ra_recv, rd_send, rd_recv):
    wide = lax.axis_index("wide")
    narrow = lax.axis_index("narrow")
    yn = wn // ROW
    y = lax.div(wide, ROW)
    g = lax.rem(wide, ROW)
    other = wide + 1 - 2 * lax.rem(wide, 2)
    cells = amp_ref.shape[1]
    blocks = cells // 128
    pairs = hole_ref.shape[0] // wn
    kt = amp_ref.shape[0] // pairs
    rows = CAP * pairs
    row_rows = ROW * rows
    parcel = room * pairs
    ki = tiles.shape[0] - 1
    share = ki // zn
    sub = share // ROW
    cells_all = NVT * NVT
    hf = cells_all // 2
    low = iota((1, 128), 1) < TILE
    y_order, z_order = far_first(yn), far_first(zn)
    mates = range(2, ROW, 2)

    def at_y(step):
        return (lax.rem(y + step, yn) * ROW + g, narrow)

    def at_g(step):
        return (y * ROW + lax.rem(g + step, ROW), narrow)

    def at_z(step):
        return (wide, lax.rem(narrow + step, zn))

    barrier = pltpu.get_barrier_semaphore()
    peers = [at_z(s) for s in z_order] + [at_y(s) for s in y_order] + [at_g(s) for s in range(1, ROW)]
    for peer in peers:
        pl.semaphore_signal(barrier, inc=1, device_id=peer, device_id_type=MESH)

    own = int_ref[...].astype(F32)
    for m in range(32):
        local32[pl.ds(m, share, stride=32), :] = own[:, m * 128:(m + 1) * 128]
    local[...] = local32[...].astype(BF16)

    owner_row = owner_ref[...]
    owner_col = column_of(owner_row)
    before = iota((kt, kt), 0) < iota((kt, kt), 1)
    count = jnp.sum(jnp.where(before & (owner_col == owner_row), 1, 0), axis=0, keepdims=True)
    slot = owner_row * CAP + count
    line = lax.div(owner_row, ROW)
    rank = jnp.sum(jnp.where(before & (lax.div(owner_col, ROW) == line), 1, 0), axis=0, keepdims=True)
    key = line * room + rank
    slot = jnp.concatenate([slot * pairs + p for p in range(pairs)], axis=1)
    key = jnp.concatenate([key * pairs + p for p in range(pairs)], axis=1)
    pick[...] = hot(iota((yn * parcel, pairs * kt), 0) == key)

    pl.semaphore_wait(barrier, len(peers))

    def part(shard, who):
        return pl.ds(pl.multiple_of((shard * share + who * sub) * 32, 16), sub * 32)

    def z_copy(step):
        return pltpu.make_async_remote_copy(
            src_ref=local.at[pl.ds(pl.multiple_of(g * sub * 32, 16), sub * 32)], dst_ref=gath.at[part(narrow, g)],
            send_sem=z_send.at[step], recv_sem=z_recv.at[step], device_id=at_z(step), device_id_type=MESH)

    def from_z(step):
        return lax.rem(narrow + zn - step, zn)

    def x_copy(step, e):
        at = gath.at[part(from_z(step), g)]
        k = step * ROW + e
        return pltpu.make_async_remote_copy(
            src_ref=at, dst_ref=at, send_sem=x_send.at[k], recv_sem=x_recv.at[k], device_id=at_g(e),
            device_id_type=MESH)

    def c_copy(step, e):
        at = gath.at[part(from_z(step), lax.rem(g + ROW - e, ROW))]
        k = step * ROW + e
        return pltpu.make_async_remote_copy(
            src_ref=at, dst_ref=at, send_sem=c_send.at[k], recv_sem=c_recv.at[k], device_id=(other, narrow),
            device_id_type=MESH)

    def spread(block, first):
        n = block.shape[0] // 32
        turned = pltpu.roll(block, TILE, 1)
        tiles[pl.ds(first, n), pl.ds(0, 32)] = jnp.where(low, block, turned).reshape(n, 32, 128)
        tiles[pl.ds(first, n), pl.ds(32, 32)] = jnp.where(low, turned, block).reshape(n, 32, 128)

    def y_copy(pack, leg, s_sem, r_sem, step):
        to = lax.rem(y + step, yn)
        return pltpu.make_async_remote_copy(
            src_ref=pack.at[pl.ds(pl.multiple_of(to * parcel, 16), parcel)],
            dst_ref=leg.at[pl.ds(step * parcel, parcel)],
            send_sem=s_sem.at[step], recv_sem=r_sem.at[step], device_id=at_y(step), device_id_type=MESH)

    def from_y(step):
        return lax.rem(y + yn - step, yn)

    def r_each(turned, recv, s_sem, r_sem, step, do):
        def one(e, c):
            k = step * ROW + e
            to = lax.rem(g + e, ROW)
            do(pltpu.make_async_remote_copy(
                src_ref=turned.at[pl.ds(pl.multiple_of(step * row_rows + to * rows, 16), rows)],
                dst_ref=recv.at[pl.ds(pl.multiple_of(from_y(step) * row_rows + g * rows, 16), rows)],
                send_sem=s_sem.at[k], recv_sem=r_sem.at[k], device_id=at_g(e), device_id_type=MESH))
            return c
        lax.fori_loop(1, ROW, one, 0)

    def forward(parcel_now, turned, recv, s_sem, r_sem, step):
        turned[pl.ds(step * row_rows, row_rows), :] = mm(order, parcel_now).astype(BF16)
        r_each(turned, recv, s_sem, r_sem, step, begin)
        mine = pl.multiple_of(g * rows, 16)
        recv[pl.ds(pl.multiple_of(from_y(step) * row_rows, 16) + mine, rows), :] = turned[
            pl.ds(step * row_rows + mine, rows), :]

    set_a = (pack_a, leg_a, ya_send, ya_recv)
    set_d = (pack_d, leg_d, yd_send, yd_recv)
    next_a = (turn_a, recv_a, ra_send, ra_recv)
    next_d = (turn_d, recv_d, rd_send, rd_recv)
    here = pl.ds(pl.multiple_of(y * parcel, 16), parcel)

    def arrive(first, second, step):
        y_copy(*first, step).wait_recv()
        forward(first[1][pl.ds(step * parcel, parcel), :], *second, step)

    for step in z_order:
        z_copy(step).start()
    pack_a[...] = mm(pick[...], amp_ref[...]).astype(BF16)
    for step in y_order:
        y_copy(*set_a, step).start()

    spread(local[...], narrow * share)
    tiles[ki] = jnp.zeros((TILE, 128), BF16)
    want = hot(iota((row_rows, pairs * kt), 0) + y * row_rows == slot)
    order = lax.dot_general(want, pick[here, :], NT, preferred_element_type=F32).astype(BF16)

    codes = codes_ref[...]
    second = lax.rem(codes, NVT)
    odd = lax.rem(second, 2)
    cell = lax.div(second, 2) * NVT + lax.div(codes, NVT)
    match = iota((hf, kt), 0) == cell
    onto = jnp.concatenate([hot(match & (odd == 0)), hot(match & (odd == 1))], axis=1)
    lows = jnp.concatenate([low] * blocks, axis=1)
    zero = jnp.zeros((kt, cells), BF16)

    def dense_pair(p):
        a = amp_ref[pl.ds(p * kt, kt), :]
        turned = jnp.concatenate([pltpu.roll(a[:, m * 128:(m + 1) * 128], TILE, 1) for m in range(blocks)], axis=1)
        g0 = mm(onto, jnp.concatenate([jnp.where(lows, a, zero), jnp.where(lows, zero, turned)], axis=0))
        g1 = mm(onto, jnp.concatenate([jnp.where(lows, turned, zero), jnp.where(lows, zero, a)], axis=0))
        for m in range(blocks):
            for h in range(NVT // 2):
                both = jnp.concatenate([v[h * NVT:(h + 1) * NVT, m * 128:(m + 1) * 128] for v in (g0, g1)], axis=0)
                adense[pl.ds((p * blocks + m) * 2 * NVT, 2 * NVT), pl.ds(h * 128, 128)] = both.astype(BF16)

    todo = list(range(pairs))
    for i, step in enumerate(z_order):
        if i % 2 == 0 and todo:
            dense_pair(todo.pop(0))
        z_copy(step).wait_recv()
        for e in mates:
            x_copy(step, e).start()
        c_copy(step, 0).start()
    for p in todo:
        dense_pair(p)
    forward(pack_a[here, :], *next_a, 0)
    for step in z_order:
        for e in mates:
            x_copy(step, e).wait_recv()
            c_copy(step, e).start()
    for step in z_order:
        for e in (0, *mates):
            c_copy(step, e).wait_recv()
        spread(gath[pl.ds(pl.multiple_of(from_z(step) * share * 32, 16), share * 32), :], from_z(step) * share)

    def gather_row(c, carry):
        for h in range(NVT // 2):
            l = tiles[table_ref[c * NVT + 2 * h]]
            r = tiles[table_ref[c * NVT + 2 * h + 1]]
            idense[pl.ds(pl.multiple_of(c * TILE, TILE), TILE), pl.ds(h * 128, 128)] = jnp.where(low, l, r)
        return carry

    lax.fori_loop(0, NVT, gather_row, 0)

    def product(n, carry):
        rhs = idense[pl.ds(pl.multiple_of(n * 256, 256), 256), :]
        d = lax.dot_general(adense[...], rhs, NT, preferred_element_type=F32)
        for p in range(pairs):
            for a in range(2 * blocks):
                x = d[(p * 2 * blocks + a) * NVT:(p * 2 * blocks + a + 1) * NVT]
                both = jnp.concatenate([x[:, :128], x[:, 128:]], axis=0).astype(BF16)
                zbuf[p, pl.ds(pl.multiple_of(n * 2 * NVT, 16), 2 * NVT), pl.ds(a * 128, 128)] = both
        return carry

    lax.fori_loop(0, NVT // 4, product, 0)

    cell_col, odd_col = column_of(cell), column_of(odd)
    match = iota((kt, hf), 1) == cell_col
    take = jnp.concatenate([hot(match & (odd_col == 0)), hot(match & (odd_col == 1))], axis=0)
    u, v = iota((512, 128), 0), iota((512, 128), 1)
    goal = ((u >> 7) & 1) * TILE + (u & 31) * 2 + ((u >> 5) & 1)
    back = hot((v == goal) & (((u >> 8) & 1) == ((u >> 6) & 1)))
    for p in range(pairs):
        got = mm(take, zbuf[p]).astype(BF16)
        for m in range(blocks):
            part_m = got[:, m * 256:(m + 1) * 256]
            flat = jnp.concatenate([part_m[:kt], part_m[kt:]], axis=1)
            dress[pl.ds(p * kt, kt), pl.ds(m * 128, 128)] = mm(flat, back).astype(BF16)
    pack_d[...] = mm(pick[...], dress[...]).astype(BF16)
    for step in y_order:
        y_copy(*set_d, step).start()

    for step in y_order:
        arrive(set_a, next_a, step)
    forward(pack_d[here, :], *next_d, 0)

    total = wn * rows
    np_all = hole_ref.shape[0]
    r0, c0 = iota((total, np_all), 0), iota((total, np_all), 1)
    by_row = mm(hot(lax.div(r0, CAP) == c0), hole_ref[...]).astype(BF16)
    r1, c1 = iota((np_all, total), 0), iota((np_all, total), 1)
    by_col = hot(lax.div(c1, rows) * pairs + lax.rem(c1, pairs) == r1)
    r2, c2 = iota((row_rows, total), 0), iota((row_rows, total), 1)
    same = lax.rem(r2, CAP) == lax.rem(lax.div(c2, pairs), CAP)
    for i in range(yn):
        hexp[pl.ds(i * row_rows, row_rows), :] = jnp.where(
            same, mm(by_row[i * row_rows:(i + 1) * row_rows], by_col), 0.0).astype(BF16)
    for step in [0] + y_order:
        r_each(*next_a, step, landed)

    def ladder(i, carry):
        at = pl.ds(pl.multiple_of(i * row_rows, 16), row_rows)
        acc[at, :] = mm(hexp[at, :], recv_a[...])
        return carry

    lax.fori_loop(0, yn, ladder, 0)

    r3, c3 = iota((row_rows, row_rows), 0), iota((row_rows, row_rows), 1)
    source = lax.div(r3, rows) * rows + lax.rem(r3, CAP) * pairs + lax.rem(lax.div(r3, CAP), pairs)
    swap = hot(c3 == source)

    def finish(step):
        r_each(*next_d, step, landed)
        at = pl.ds(pl.multiple_of(from_y(step) * row_rows, 16), row_rows)
        done = (acc[at, :] + mm(swap, recv_d[at, :])).astype(BF16)
        out_ref[pl.ds(from_y(step) * ROW * pairs, ROW * pairs)] = done.reshape(ROW * pairs, CAP, cells)

    waiting = [0]
    for step in y_order:
        arrive(set_d, next_d, step)
        finish(waiting.pop())
        waiting.append(step)
    finish(waiting.pop())

    for step in z_order:
        z_copy(step).wait_send()
        c_copy(step, 0).wait_send()
        for e in mates:
            x_copy(step, e).wait_send()
            c_copy(step, e).wait_send()
    for step in y_order:
        y_copy(*set_a, step).wait_send()
        y_copy(*set_d, step).wait_send()
    for step in [0] + y_order:
        r_each(*next_a, step, left)
        r_each(*next_d, step, left)


def run(wn, zn, number, room, table, amps, ints, hole, codes, owner):
    cells = amps.shape[1]
    share = ints.shape[0]
    ki = share * zn
    pairs = hole.shape[0] // wn
    total = wn * CAP * pairs
    yn = wn // ROW
    blocks = cells // 128
    packed = yn * room * pairs
    vmem = pl.BlockSpec(memory_space=pltpu.VMEM)
    dma = pltpu.SemaphoreType.DMA
    return pl.pallas_call(
        functools.partial(kernel, wn, zn, room),
        out_shape=jax.ShapeDtypeStruct((wn * pairs, CAP, cells), BF16),
        in_specs=[pl.BlockSpec(memory_space=pltpu.SMEM)] + [vmem] * 5,
        out_specs=vmem,
        scratch_shapes=[
            pltpu.VMEM((share * 32, 128), BF16),
            pltpu.VMEM((share * 32, 128), F32),
            pltpu.VMEM((ki * 32, 128), BF16),
            pltpu.VMEM((ki + 1, TILE, 128), BF16),
            pltpu.VMEM((NVT * TILE, NVT * TILE), BF16),
            pltpu.VMEM((pairs * blocks * 2 * NVT, NVT * TILE), BF16),
            pltpu.VMEM((pairs, NVT * NVT // 2, 2 * cells), BF16),
            pltpu.VMEM(amps.shape, BF16),
            pltpu.VMEM((packed, amps.shape[0]), BF16),
        ] + [pltpu.VMEM((packed, cells), BF16)] * 4 + [pltpu.VMEM((total, cells), BF16)] * 4 + [
            pltpu.VMEM((total, total), BF16),
            pltpu.VMEM((total, cells), F32),
        ] + [dma((zn,))] * 2 + [dma((zn * ROW,))] * 4 + [dma((yn,))] * 4 + [dma((yn * ROW,))] * 4,
        compiler_params=pltpu.CompilerParams(
            collective_id=number, has_side_effects=True, vmem_limit_bytes=58 * 1024 * 1024
        ),
        cost_estimate=pl.CostEstimate(flops=8 * 10**9, bytes_accessed=4 * 10**6, transcendentals=0),
    )(table, amps, ints, hole, codes, owner)


def per_device(wn, zn, amplitudes, int_values, hole_ladder, amp_tiles, int_tiles, owner):
    pairs, kt, cells = amplitudes.shape
    ki = int_values.shape[0] * zn
    yn = wn // ROW
    matches = jnp.arange(NVT * NVT, dtype=I32)[:, None] == int_tiles[None, :]
    table = ki + jnp.sum(jnp.where(matches, jnp.arange(ki, dtype=I32)[None, :] - ki, 0), axis=1)
    fill = jnp.sum((owner // ROW == jnp.arange(yn, dtype=I32)[None, :]).astype(I32), axis=0)
    most = jnp.max(fill)
    rooms = tuple(r * ROW * CAP // 32 for r in ROOMS)
    branch = sum((most > r).astype(I32) for r in rooms[:-1])
    return lax.switch(
        branch,
        [functools.partial(run, wn, zn, i, room) for i, room in enumerate(rooms)],
        table,
        amplitudes.reshape(pairs * kt, cells),
        int_values,
        hole_ladder,
        amp_tiles.reshape(1, kt),
        owner.reshape(1, kt),
    )


def solution(mesh):
    wn, zn = mesh.shape["wide"], mesh.shape["narrow"]
    return jax.shard_map(
        functools.partial(per_device, wn, zn),
        mesh=mesh,
        in_specs=(P("wide", None, "narrow"), P("narrow", None), P(), P(), P(), P()),
        out_specs=P(None, "wide", "narrow"),
        check_vma=False,
    )
```

```python
import functools

import jax
import jax.numpy as jnp
from jax import lax
from jax.experimental import pallas as pl
from jax.experimental.pallas import tpu as pltpu
from jax.sharding import PartitionSpec as P

TILE = 64
NVT = 24
CAP = 4
ROW = 8
ROOMS = (20, 24, 32)
MESH = pl.DeviceIdType.MESH
NT = (((1,), (1,)), ((), ()))
BF16, F32, I32 = jnp.bfloat16, jnp.float32, jnp.int32


def iota(shape, dim):
    return lax.broadcasted_iota(I32, shape, dim)


def hot(mask):
    return jnp.where(mask, 1.0, 0.0).astype(BF16)


def mm(a, b):
    return jnp.dot(a, b, preferred_element_type=F32)


def column_of(row):
    n = row.shape[1]
    eye = iota((n, n), 0) == iota((n, n), 1)
    return jnp.sum(jnp.where(eye, row, 0), axis=1, keepdims=True)


def near_first(n):
    return sorted(range(1, n), key=lambda d: (min(d, n - d), d))


def kernel(wn, zn, room, table_ref, amp_ref, int_ref, hole_ref, codes_ref, owner_ref, out_ref,
           local, local32, gath, tiles, idense, adense, zbuf, dress, pick, pack_a, pack_d, leg_a, leg_d,
           turn_a, turn_d, stage_a, stage_d, recv_a, recv_d, hexp, acc,
           z_send, z_recv, x_send, x_recv, c_send, c_recv, ya_send, ya_recv, yd_send, yd_recv,
           ra_send, ra_recv, rd_send, rd_recv, ca_send, ca_recv, cd_send, cd_recv):
    wide = lax.axis_index("wide")
    narrow = lax.axis_index("narrow")
    yn = wn // ROW
    y = lax.div(wide, ROW)
    g = lax.rem(wide, ROW)
    other = wide + 1 - 2 * lax.rem(wide, 2)
    cells = amp_ref.shape[1]
    blocks = cells // 128
    pairs = hole_ref.shape[0] // wn
    kt = amp_ref.shape[0] // pairs
    rows = CAP * pairs
    row_rows = ROW * rows
    parcel = room * pairs
    ki = tiles.shape[0] - 1
    share = ki // zn
    sub = share // ROW
    cells_all = NVT * NVT
    hf = cells_all // 2
    low = iota((1, 128), 1) < TILE
    y_order, z_order = near_first(yn), near_first(zn)
    mates = range(2, ROW, 2)

    def at_y(step):
        return (lax.rem(y + step, yn) * ROW + g, narrow)

    def at_g(step):
        return (y * ROW + lax.rem(g + step, ROW), narrow)

    def at_z(step):
        return (wide, lax.rem(narrow + step, zn))

    barrier = pltpu.get_barrier_semaphore()
    peers = [at_z(s) for s in z_order] + [at_y(s) for s in y_order] + [at_g(s) for s in range(1, ROW)]
    for peer in peers:
        pl.semaphore_signal(barrier, inc=1, device_id=peer, device_id_type=MESH)

    own = int_ref[...].astype(F32)
    for m in range(32):
        local32[pl.ds(m, share, stride=32), :] = own[:, m * 128:(m + 1) * 128]
    local[...] = local32[...].astype(BF16)

    owner_row = owner_ref[...]
    owner_col = column_of(owner_row)
    before = iota((kt, kt), 0) < iota((kt, kt), 1)
    count = jnp.sum(jnp.where(before & (owner_col == owner_row), 1, 0), axis=0, keepdims=True)
    slot = owner_row * CAP + count
    line = lax.div(owner_row, ROW)
    rank = jnp.sum(jnp.where(before & (lax.div(owner_col, ROW) == line), 1, 0), axis=0, keepdims=True)
    key = line * room + rank
    slot = jnp.concatenate([slot * pairs + p for p in range(pairs)], axis=1)
    key = jnp.concatenate([key * pairs + p for p in range(pairs)], axis=1)
    pick[...] = hot(iota((yn * parcel, pairs * kt), 0) == key)

    pl.semaphore_wait(barrier, len(peers))

    def part(shard, who):
        return pl.ds(pl.multiple_of((shard * share + who * sub) * 32, 16), sub * 32)

    def z_copy(step):
        return pltpu.make_async_remote_copy(
            src_ref=local.at[pl.ds(pl.multiple_of(g * sub * 32, 16), sub * 32)], dst_ref=gath.at[part(narrow, g)],
            send_sem=z_send.at[step], recv_sem=z_recv.at[step], device_id=at_z(step), device_id_type=MESH)

    def from_z(step):
        return lax.rem(narrow + zn - step, zn)

    def x_copy(step, e):
        at = gath.at[part(from_z(step), g)]
        k = step * ROW + e
        return pltpu.make_async_remote_copy(
            src_ref=at, dst_ref=at, send_sem=x_send.at[k], recv_sem=x_recv.at[k], device_id=at_g(e),
            device_id_type=MESH)

    def c_copy(step, e):
        at = gath.at[part(from_z(step), lax.rem(g + ROW - e, ROW))]
        k = step * ROW + e
        return pltpu.make_async_remote_copy(
            src_ref=at, dst_ref=at, send_sem=c_send.at[k], recv_sem=c_recv.at[k], device_id=(other, narrow),
            device_id_type=MESH)

    def spread(block, first):
        n = block.shape[0] // 32
        turned = pltpu.roll(block, TILE, 1)
        tiles[pl.ds(first, n), pl.ds(0, 32)] = jnp.where(low, block, turned).reshape(n, 32, 128)
        tiles[pl.ds(first, n), pl.ds(32, 32)] = jnp.where(low, turned, block).reshape(n, 32, 128)

    def y_copy(pack, leg, s_sem, r_sem, step):
        to = lax.rem(y + step, yn)
        return pltpu.make_async_remote_copy(
            src_ref=pack.at[pl.ds(pl.multiple_of(to * parcel, 16), parcel)],
            dst_ref=leg.at[pl.ds(step * parcel, parcel)],
            send_sem=s_sem.at[step], recv_sem=r_sem.at[step], device_id=at_y(step), device_id_type=MESH)

    def from_y(step):
        return lax.rem(y + yn - step, yn)

    def r_copy(turned, stage, recv, r_s, r_r, c_s, c_r, step, e):
        k = step * ROW + e
        to = lax.div(lax.rem(g + e, ROW), 2)
        return pltpu.make_async_remote_copy(
            src_ref=turned.at[pl.ds(pl.multiple_of(step * row_rows + to * 2 * rows, 16), 2 * rows)],
            dst_ref=stage.at[pl.ds(k * rows, 2 * rows)],
            send_sem=r_s.at[k], recv_sem=r_r.at[k], device_id=at_g(e), device_id_type=MESH)

    def h_copy(turned, stage, recv, r_s, r_r, c_s, c_r, step, e):
        k = step * ROW + e
        if e == 0:
            src = turned.at[pl.ds(pl.multiple_of(step * row_rows + lax.rem(other, ROW) * rows, 16), rows)]
        else:
            src = stage.at[pl.ds(pl.multiple_of(k * rows + lax.rem(other, 2) * rows, 16), rows)]
        return pltpu.make_async_remote_copy(
            src_ref=src, dst_ref=recv.at[recv_at(step, e)],
            send_sem=c_s.at[k], recv_sem=c_r.at[k], device_id=(other, narrow), device_id_type=MESH)

    def recv_at(step, e):
        return pl.ds(pl.multiple_of(from_y(step) * row_rows + lax.rem(g + ROW - e, ROW) * rows, 16), rows)

    def forward(parcel_now, step, turned, stage, recv, *sems):
        turned[pl.ds(step * row_rows, row_rows), :] = mm(order, parcel_now).astype(BF16)
        for e in mates:
            r_copy(turned, stage, recv, *sems, step, e).start()
        h_copy(turned, stage, recv, *sems, step, 0).start()
        recv[recv_at(step, 0), :] = turned[pl.ds(pl.multiple_of(step * row_rows + g * rows, 16), rows), :]

    def relay(step, turned, stage, recv, *sems):
        for e in mates:
            r_copy(turned, stage, recv, *sems, step, e).wait_recv()
            h_copy(turned, stage, recv, *sems, step, e).start()
            at = pl.multiple_of((step * ROW + e) * rows + lax.rem(g, 2) * rows, 16)
            recv[recv_at(step, e), :] = stage[pl.ds(at, rows), :]

    def settle(step, *second):
        for e in (0, *mates):
            h_copy(*second, step, e).wait_recv()

    set_a = (pack_a, leg_a, ya_send, ya_recv)
    set_d = (pack_d, leg_d, yd_send, yd_recv)
    next_a = (turn_a, stage_a, recv_a, ra_send, ra_recv, ca_send, ca_recv)
    next_d = (turn_d, stage_d, recv_d, rd_send, rd_recv, cd_send, cd_recv)
    here = pl.ds(pl.multiple_of(y * parcel, 16), parcel)

    def arrive(step, first, second):
        y_copy(*first, step).wait_recv()
        forward(first[1][pl.ds(step * parcel, parcel), :], step, *second)

    for step in z_order:
        z_copy(step).start()
    pack_a[...] = mm(pick[...], amp_ref[...]).astype(BF16)
    for step in y_order:
        y_copy(*set_a, step).start()

    spread(local[...], narrow * share)
    tiles[ki] = jnp.zeros((TILE, 128), BF16)
    want = hot(iota((row_rows, pairs * kt), 0) + y * row_rows == slot)
    order = lax.dot_general(want, pick[here, :], NT, preferred_element_type=F32).astype(BF16)

    codes = codes_ref[...]
    second = lax.rem(codes, NVT)
    odd = lax.rem(second, 2)
    cell = lax.div(second, 2) * NVT + lax.div(codes, NVT)
    match = iota((hf, kt), 0) == cell
    onto = jnp.concatenate([hot(match & (odd == 0)), hot(match & (odd == 1))], axis=1)
    lows = jnp.concatenate([low] * blocks, axis=1)
    zero = jnp.zeros((kt, cells), BF16)

    def dense_pair(p):
        a = amp_ref[pl.ds(p * kt, kt), :]
        turned = jnp.concatenate([pltpu.roll(a[:, m * 128:(m + 1) * 128], TILE, 1) for m in range(blocks)], axis=1)
        g0 = mm(onto, jnp.concatenate([jnp.where(lows, a, zero), jnp.where(lows, zero, turned)], axis=0))
        g1 = mm(onto, jnp.concatenate([jnp.where(lows, turned, zero), jnp.where(lows, zero, a)], axis=0))
        for m in range(blocks):
            for h in range(NVT // 2):
                both = jnp.concatenate([v[h * NVT:(h + 1) * NVT, m * 128:(m + 1) * 128] for v in (g0, g1)], axis=0)
                adense[pl.ds((p * blocks + m) * 2 * NVT, 2 * NVT), pl.ds(h * 128, 128)] = both.astype(BF16)

    todo = list(range(pairs))
    for i, step in enumerate(z_order):
        if i % 2 == 0 and todo:
            dense_pair(todo.pop(0))
        z_copy(step).wait_recv()
        for e in mates:
            x_copy(step, e).start()
        c_copy(step, 0).start()
        if i >= 2:
            for e in mates:
                x_copy(z_order[i - 2], e).wait_recv()
                c_copy(z_order[i - 2], e).start()
    for p in todo:
        dense_pair(p)
    for step in z_order[-2:]:
        for e in mates:
            x_copy(step, e).wait_recv()
            c_copy(step, e).start()
    forward(pack_a[here, :], 0, *next_a)
    early = (len(y_order) + 1) // 2
    coming, going = y_order[:early], [0]
    for step in z_order:
        if coming:
            arrive(coming[0], set_a, next_a)
            going.append(coming.pop(0))
        for e in (0, *mates):
            c_copy(step, e).wait_recv()
        spread(gath[pl.ds(pl.multiple_of(from_z(step) * share * 32, 16), share * 32), :], from_z(step) * share)
    for step in coming:
        arrive(step, set_a, next_a)
        going.append(step)
    coming = y_order[early:]

    def gather_row(c, carry):
        for h in range(NVT // 2):
            l = tiles[table_ref[0, c * NVT + 2 * h]]
            r = tiles[table_ref[0, c * NVT + 2 * h + 1]]
            idense[pl.ds(pl.multiple_of(c * TILE, TILE), TILE), pl.ds(h * 128, 128)] = jnp.where(low, l, r)
        return carry

    lax.fori_loop(0, NVT, gather_row, 0)

    def product(n, carry):
        rhs = idense[pl.ds(pl.multiple_of(n * 256, 256), 256), :]
        d = lax.dot_general(adense[...], rhs, NT, preferred_element_type=F32)
        for p in range(pairs):
            for a in range(2 * blocks):
                x = d[(p * 2 * blocks + a) * NVT:(p * 2 * blocks + a + 1) * NVT]
                both = jnp.concatenate([x[:, :128], x[:, 128:]], axis=0).astype(BF16)
                zbuf[p, pl.ds(pl.multiple_of(n * 2 * NVT, 16), 2 * NVT), pl.ds(a * 128, 128)] = both
        return carry

    lax.fori_loop(0, NVT // 8, product, 0)
    for step in going:
        relay(step, *next_a)
    lax.fori_loop(NVT // 8, NVT // 4, product, 0)
    for step in coming:
        arrive(step, set_a, next_a)

    cell_col, odd_col = column_of(cell), column_of(odd)
    match = iota((kt, hf), 1) == cell_col
    take = jnp.concatenate([hot(match & (odd_col == 0)), hot(match & (odd_col == 1))], axis=0)
    u, v = iota((512, 128), 0), iota((512, 128), 1)
    goal = ((u >> 7) & 1) * TILE + (u & 31) * 2 + ((u >> 5) & 1)
    back = hot((v == goal) & (((u >> 8) & 1) == ((u >> 6) & 1)))
    for p in range(pairs):
        got = mm(take, zbuf[p]).astype(BF16)
        for m in range(blocks):
            part_m = got[:, m * 256:(m + 1) * 256]
            flat = jnp.concatenate([part_m[:kt], part_m[kt:]], axis=1)
            dress[pl.ds(p * kt, kt), pl.ds(m * 128, 128)] = mm(flat, back).astype(BF16)
    pack_d[...] = mm(pick[...], dress[...]).astype(BF16)
    for step in y_order:
        y_copy(*set_d, step).start()

    for step in coming:
        relay(step, *next_a)
    forward(pack_d[here, :], 0, *next_d)

    total = wn * rows
    np_all = hole_ref.shape[0]
    r0, c0 = iota((total, np_all), 0), iota((total, np_all), 1)
    by_row = mm(hot(lax.div(r0, CAP) == c0), hole_ref[...]).astype(BF16)
    r1, c1 = iota((np_all, total), 0), iota((np_all, total), 1)
    by_col = hot(lax.div(c1, rows) * pairs + lax.rem(c1, pairs) == r1)
    r2, c2 = iota((row_rows, total), 0), iota((row_rows, total), 1)
    same = lax.rem(r2, CAP) == lax.rem(lax.div(c2, pairs), CAP)
    for i in range(yn):
        hexp[pl.ds(i * row_rows, row_rows), :] = jnp.where(
            same, mm(by_row[i * row_rows:(i + 1) * row_rows], by_col), 0.0).astype(BF16)
    for step in [0] + y_order:
        settle(step, *next_a)

    def ladder(i, carry):
        at = pl.ds(pl.multiple_of(i * row_rows, 16), row_rows)
        acc[at, :] = mm(hexp[at, :], recv_a[...])
        return carry

    lax.fori_loop(0, yn, ladder, 0)

    r3, c3 = iota((row_rows, row_rows), 0), iota((row_rows, row_rows), 1)
    source = lax.div(r3, rows) * rows + lax.rem(r3, CAP) * pairs + lax.rem(lax.div(r3, CAP), pairs)
    swap = hot(c3 == source)

    def finish(step):
        settle(step, *next_d)
        at = pl.ds(pl.multiple_of(from_y(step) * row_rows, 16), row_rows)
        done = (acc[at, :] + mm(swap, recv_d[at, :])).astype(BF16)
        out_ref[pl.ds(from_y(step) * ROW * pairs, ROW * pairs)] = done.reshape(ROW * pairs, CAP, cells)

    line_up = [0] + y_order
    for i, step in enumerate(line_up):
        if i >= 1:
            arrive(step, set_d, next_d)
            relay(line_up[i - 1], *next_d)
        if i >= 2:
            finish(line_up[i - 2])
    relay(line_up[-1], *next_d)
    for step in line_up[-2:]:
        finish(step)

    for step in z_order:
        z_copy(step).wait_send()
        c_copy(step, 0).wait_send()
        for e in mates:
            x_copy(step, e).wait_send()
            c_copy(step, e).wait_send()
    for step in y_order:
        y_copy(*set_a, step).wait_send()
        y_copy(*set_d, step).wait_send()
    for step in [0] + y_order:
        for second in (next_a, next_d):
            h_copy(*second, step, 0).wait_send()
            for e in mates:
                r_copy(*second, step, e).wait_send()
                h_copy(*second, step, e).wait_send()


def prepare(wn, rooms, codes_ref, owner_ref, table_ref, branch_ref):
    ki, kt = codes_ref.shape[1], owner_ref.shape[1]
    codes = column_of(codes_ref[...])
    found = codes == iota((ki, NVT * NVT), 1)
    table_ref[...] = ki + jnp.sum(jnp.where(found, iota((ki, NVT * NVT), 0) - ki, 0), axis=0, keepdims=True)
    line = lax.div(owner_ref[...], ROW)
    fill = jnp.sum(jnp.where(line == iota((wn // ROW, kt), 0), 1, 0), axis=1, keepdims=True)
    most = jnp.max(fill, axis=0, keepdims=True)
    branch_ref[...] = sum(jnp.where(most > r, 1, 0) for r in rooms[:-1])


def run(wn, zn, number, room, table, amps, ints, hole, codes, owner):
    cells = amps.shape[1]
    share = ints.shape[0]
    ki = share * zn
    pairs = hole.shape[0] // wn
    total = wn * CAP * pairs
    yn = wn // ROW
    blocks = cells // 128
    packed = yn * room * pairs
    vmem = pl.BlockSpec(memory_space=pltpu.VMEM)
    dma = pltpu.SemaphoreType.DMA
    return pl.pallas_call(
        functools.partial(kernel, wn, zn, room),
        out_shape=jax.ShapeDtypeStruct((wn * pairs, CAP, cells), BF16),
        in_specs=[pl.BlockSpec(memory_space=pltpu.SMEM)] + [vmem] * 5,
        out_specs=vmem,
        scratch_shapes=[
            pltpu.VMEM((share * 32, 128), BF16),
            pltpu.VMEM((share * 32, 128), F32),
            pltpu.VMEM((ki * 32, 128), BF16),
            pltpu.VMEM((ki + 1, TILE, 128), BF16),
            pltpu.VMEM((NVT * TILE, NVT * TILE), BF16),
            pltpu.VMEM((pairs * blocks * 2 * NVT, NVT * TILE), BF16),
            pltpu.VMEM((pairs, NVT * NVT // 2, 2 * cells), BF16),
            pltpu.VMEM(amps.shape, BF16),
            pltpu.VMEM((packed, amps.shape[0]), BF16),
        ] + [pltpu.VMEM((packed, cells), BF16)] * 4 + [pltpu.VMEM((total, cells), BF16)] * 6 + [
            pltpu.VMEM((total, total), BF16),
            pltpu.VMEM((total, cells), F32),
        ] + [dma((zn,))] * 2 + [dma((zn * ROW,))] * 4 + [dma((yn,))] * 4 + [dma((yn * ROW,))] * 8,
        compiler_params=pltpu.CompilerParams(
            collective_id=number, has_side_effects=True, vmem_limit_bytes=58 * 1024 * 1024
        ),
        cost_estimate=pl.CostEstimate(flops=8 * 10**9, bytes_accessed=4 * 10**6, transcendentals=0),
    )(table, amps, ints, hole, codes, owner)


def per_device(wn, zn, amplitudes, int_values, hole_ladder, amp_tiles, int_tiles, owner):
    pairs, kt, cells = amplitudes.shape
    ki = int_values.shape[0] * zn
    rooms = tuple(r * ROW * CAP // 32 for r in ROOMS)
    codes, owner = int_tiles.reshape(1, ki), owner.reshape(1, kt)
    table, branch = pl.pallas_call(
        functools.partial(prepare, wn, rooms),
        out_shape=(jax.ShapeDtypeStruct((1, NVT * NVT), I32), jax.ShapeDtypeStruct((1, 1), I32)),
        in_specs=[pl.BlockSpec(memory_space=pltpu.VMEM)] * 2,
        out_specs=(pl.BlockSpec(memory_space=pltpu.VMEM), pl.BlockSpec(memory_space=pltpu.VMEM)),
    )(codes, owner)
    return lax.switch(
        branch[0, 0],
        [functools.partial(run, wn, zn, i, room) for i, room in enumerate(rooms)],
        table,
        amplitudes.reshape(pairs * kt, cells),
        int_values,
        hole_ladder,
        amp_tiles.reshape(1, kt),
        owner,
    )


def solution(mesh):
    wn, zn = mesh.shape["wide"], mesh.shape["narrow"]
    return jax.shard_map(
        functools.partial(per_device, wn, zn),
        mesh=mesh,
        in_specs=(P("wide", None, "narrow"), P("narrow", None), P(), P(), P(), P()),
        out_specs=P(None, "wide", "narrow"),
        check_vma=False,
    )
```

```python
import functools

import jax
import jax.numpy as jnp
from jax import lax
from jax.experimental import pallas as pl
from jax.experimental.pallas import tpu as pltpu
from jax.sharding import PartitionSpec as P

TILE = 64
NVT = 24
CAP = 4
MESH = pl.DeviceIdType.MESH
NT = (((1,), (1,)), ((), ()))
BF16, F32, I32 = jnp.bfloat16, jnp.float32, jnp.int32


def iota(shape, dim):
    return lax.broadcasted_iota(I32, shape, dim)


def hot(mask):
    return jnp.where(mask, 1.0, 0.0).astype(BF16)


def mm(a, b):
    return jnp.dot(a, b, preferred_element_type=F32)


def column_of(row):
    n = row.shape[1]
    eye = iota((n, n), 0) == iota((n, n), 1)
    return jnp.sum(jnp.where(eye, row, 0), axis=1, keepdims=True)


def near_first(n):
    return sorted(range(1, n), key=lambda d: (min(d, n - d), d))


def kernel(wn, zn, listed_ref, amp_ref, int_ref, hole_ref, codes_ref, owner_ref, out_ref,
           local, local32, gath, tiles, idense, adense, zbuf, dress, pick, send_a, send_d, recv_a, recv_d, hexp, acc,
           table_vec, table_ref, table_sem, z_send, z_recv, c_send, c_recv, a_send, a_recv, d_send, d_recv):
    wide = lax.axis_index("wide")
    narrow = lax.axis_index("narrow")
    core = lax.rem(wide, 2)
    other = wide + 1 - 2 * core
    cells = amp_ref.shape[1]
    blocks = cells // 128
    pairs = hole_ref.shape[0] // wn
    kt = amp_ref.shape[0] // pairs
    rows = CAP * pairs
    total = wn * rows
    part_rows = 8 * rows if wn % 8 == 0 else total
    ki = tiles.shape[0] - 1
    share = ki // zn
    half_rows = share * 16
    cells_all = NVT * NVT
    hf = cells_all // 2
    low = iota((1, 128), 1) < TILE
    z_order = near_first(zn)
    relays = {d: (2 if d == 3 else zn - 2) for d in z_order if min(d, zn - d) == 3}

    def at_z(step):
        return (wide, lax.rem(narrow + step, zn))

    barrier = pltpu.get_barrier_semaphore()
    peers = [d for d in z_order if d not in relays]
    for step in peers:
        pl.semaphore_signal(barrier, inc=1, device_id=at_z(step), device_id_type=MESH)

    def greet(i, c):
        pl.semaphore_signal(barrier, inc=1, device_id=(lax.rem(wide + i, wn), narrow), device_id_type=MESH)
        return c

    lax.fori_loop(1, wn, greet, 0)

    own = int_ref[...].astype(F32)
    for m in range(32):
        local32[pl.ds(m, share, stride=32), :] = own[:, m * 128:(m + 1) * 128]
    local[...] = local32[...].astype(BF16)

    owner_row = owner_ref[...]
    owner_col = column_of(owner_row)
    before = iota((kt, kt), 0) < iota((kt, kt), 1)
    count = jnp.sum(jnp.where(before & (owner_col == owner_row), 1, 0), axis=0, keepdims=True)
    slot = (owner_row * CAP + count) * pairs
    slot = jnp.concatenate([slot + p for p in range(pairs)], axis=1)
    pick[...] = hot(iota((total, pairs * kt), 0) == slot)

    pl.semaphore_wait(barrier, len(peers) + wn - 1)

    def half(shard, who):
        return pl.ds(pl.multiple_of(shard * share * 32 + who * half_rows, 16), half_rows)

    def from_z(step):
        return lax.rem(narrow + zn - step, zn)

    def z_copy(step):
        if step in relays:
            src, to = gath.at[half(from_z(relays[step]), core)], at_z(step - relays[step] + zn)
            dst = gath.at[half(from_z(relays[step]), core)]
        else:
            src, to = local.at[pl.ds(pl.multiple_of(core * half_rows, 16), half_rows)], at_z(step)
            dst = gath.at[half(narrow, core)]
        return pltpu.make_async_remote_copy(
            src_ref=src, dst_ref=dst, send_sem=z_send.at[step], recv_sem=z_recv.at[step], device_id=to,
            device_id_type=MESH)

    def c_copy(step):
        at = gath.at[half(from_z(step), core)]
        return pltpu.make_async_remote_copy(
            src_ref=at, dst_ref=at, send_sem=c_send.at[step], recv_sem=c_recv.at[step], device_id=(other, narrow),
            device_id_type=MESH)

    def spread(block, first):
        n = block.shape[0] // 32
        turned = pltpu.roll(block, TILE, 1)
        tiles[pl.ds(first, n), pl.ds(0, 32)] = jnp.where(low, block, turned).reshape(n, 32, 128)
        tiles[pl.ds(first, n), pl.ds(32, 32)] = jnp.where(low, turned, block).reshape(n, 32, 128)

    def spread_half(step, who):
        spread(gath[half(from_z(step), who), :], from_z(step) * share + who * (share // 2))

    def post(send, recv, s_sem, r_sem, do):
        def one(i, c):
            i = lax.rem(i + 3 * wn // 8, wn - 1) + 1
            to = lax.rem(wide + i, wn)
            do(pltpu.make_async_remote_copy(
                src_ref=send.at[pl.ds(pl.multiple_of(to * rows, 16), rows)],
                dst_ref=recv.at[pl.ds(pl.multiple_of(wide * rows, 16), rows)],
                send_sem=s_sem.at[i], recv_sem=r_sem.at[i], device_id=(to, narrow), device_id_type=MESH))
            return c
        lax.fori_loop(0, wn - 1, one, 0)

    set_a = (send_a, recv_a, a_send, a_recv)
    set_d = (send_d, recv_d, d_send, d_recv)
    mine = pl.ds(pl.multiple_of(wide * rows, 16), rows)

    twos = [d for d in peers if d in relays.values()]
    for step in twos:
        z_copy(step).start()
    send_a[...] = mm(pick[...], amp_ref[...]).astype(BF16)
    post(*set_a, lambda copy: copy.start())
    for step in peers:
        if step not in twos:
            z_copy(step).start()
    recv_a[mine] = send_a[mine]

    spread(local[...], narrow * share)
    tiles[ki] = jnp.zeros((TILE, 128), BF16)

    codes = codes_ref[...]
    second = lax.rem(codes, NVT)
    odd = lax.rem(second, 2)
    cell = lax.div(second, 2) * NVT + lax.div(codes, NVT)
    match = iota((hf, kt), 0) == cell
    onto = jnp.concatenate([hot(match & (odd == 0)), hot(match & (odd == 1))], axis=1)
    lows = jnp.concatenate([low] * blocks, axis=1)
    zero = jnp.zeros((kt, cells), BF16)

    def dense_pair(p):
        a = amp_ref[pl.ds(p * kt, kt), :]
        turned = jnp.concatenate([pltpu.roll(a[:, m * 128:(m + 1) * 128], TILE, 1) for m in range(blocks)], axis=1)
        g0 = mm(onto, jnp.concatenate([jnp.where(lows, a, zero), jnp.where(lows, zero, turned)], axis=0))
        g1 = mm(onto, jnp.concatenate([jnp.where(lows, turned, zero), jnp.where(lows, zero, a)], axis=0))
        for m in range(blocks):
            for h in range(NVT // 2):
                both = jnp.concatenate([v[h * NVT:(h + 1) * NVT, m * 128:(m + 1) * 128] for v in (g0, g1)], axis=0)
                adense[pl.ds((p * blocks + m) * 2 * NVT, 2 * NVT), pl.ds(h * 128, 128)] = both.astype(BF16)

    found = column_of(listed_ref[...]) == iota((ki, cells_all), 1)
    last = jnp.max(jnp.where(found, iota((ki, cells_all), 0), -1), axis=0, keepdims=True)
    table_vec[...] = jnp.where(last < 0, ki, last)
    to_scalar = pltpu.make_async_copy(table_vec, table_ref, table_sem)
    to_scalar.start()
    for p in range(pairs):
        dense_pair(p)
    to_scalar.wait()
    for step in twos:
        z_copy(step).wait_recv()
        for d in relays:
            if relays[d] == step:
                z_copy(d).start()
        c_copy(step).start()
    for step in z_order:
        if step not in twos:
            z_copy(step).wait_recv()
            c_copy(step).start()
            spread_half(step, core)
    for step in twos:
        spread_half(step, core)
    for step in z_order:
        c_copy(step).wait_recv()
        spread_half(step, 1 - core)

    def gather_rows(n):
        for c in range(4):
            for h in range(NVT // 2):
                l = tiles[table_ref[0, (n * 4 + c) * NVT + 2 * h]]
                r = tiles[table_ref[0, (n * 4 + c) * NVT + 2 * h + 1]]
                idense[pl.ds(pl.multiple_of(n * 256 + c * TILE, TILE), TILE), pl.ds(h * 128, 128)] = jnp.where(
                    low, l, r)

    gather_rows(0)

    def product(n, carry):
        rhs = idense[pl.ds(pl.multiple_of(n * 256, 256), 256), :]
        d = lax.dot_general(adense[...], rhs, NT, preferred_element_type=F32)
        gather_rows(lax.rem(n + 1, NVT // 4))
        for p in range(pairs):
            for a in range(2 * blocks):
                x = d[(p * 2 * blocks + a) * NVT:(p * 2 * blocks + a + 1) * NVT]
                both = jnp.concatenate([x[:, :128], x[:, 128:]], axis=0).astype(BF16)
                zbuf[p, pl.ds(pl.multiple_of(n * 2 * NVT, 16), 2 * NVT), pl.ds(a * 128, 128)] = both
        return carry

    lax.fori_loop(0, NVT // 4, product, 0)

    cell_col, odd_col = column_of(cell), column_of(odd)
    match = iota((kt, hf), 1) == cell_col
    take = jnp.concatenate([hot(match & (odd_col == 0)), hot(match & (odd_col == 1))], axis=0)
    u, v = iota((512, 128), 0), iota((512, 128), 1)
    goal = ((u >> 7) & 1) * TILE + (u & 31) * 2 + ((u >> 5) & 1)
    back = hot((v == goal) & (((u >> 8) & 1) == ((u >> 6) & 1)))
    for p in range(pairs):
        got = mm(take, zbuf[p]).astype(BF16)
        for m in range(blocks):
            part_m = got[:, m * 256:(m + 1) * 256]
            flat = jnp.concatenate([part_m[:kt], part_m[kt:]], axis=1)
            dress[pl.ds(p * kt, kt), pl.ds(m * 128, 128)] = mm(flat, back).astype(BF16)
    send_d[...] = mm(pick[...], dress[...]).astype(BF16)
    post(*set_d, lambda copy: copy.start())
    recv_d[mine] = send_d[mine]

    np_all = hole_ref.shape[0]
    r0, c0 = iota((total, np_all), 0), iota((total, np_all), 1)
    by_row = mm(hot(lax.div(r0, CAP) == c0), hole_ref[...]).astype(BF16)
    r1, c1 = iota((np_all, total), 0), iota((np_all, total), 1)
    by_col = hot(lax.div(c1, rows) * pairs + lax.rem(c1, pairs) == r1)
    r2, c2 = iota((part_rows, total), 0), iota((part_rows, total), 1)
    same = lax.rem(r2, CAP) == lax.rem(lax.div(c2, pairs), CAP)
    for i in range(total // part_rows):
        hexp[pl.ds(i * part_rows, part_rows), :] = jnp.where(
            same, mm(by_row[i * part_rows:(i + 1) * part_rows], by_col), 0.0).astype(BF16)
    post(*set_a, lambda copy: copy.wait_recv())

    def ladder(i, carry):
        at = pl.ds(pl.multiple_of(i * part_rows, 16), part_rows)
        acc[at, :] = mm(hexp[at, :], recv_a[...])
        return carry

    lax.fori_loop(0, total // part_rows, ladder, 0)

    r3, c3 = iota((part_rows, part_rows), 0), iota((part_rows, part_rows), 1)
    source = lax.div(r3, rows) * rows + lax.rem(r3, CAP) * pairs + lax.rem(lax.div(r3, CAP), pairs)
    swap = hot(c3 == source)

    post(*set_d, lambda copy: copy.wait_recv())

    def finish(i, carry):
        at = pl.ds(pl.multiple_of(i * part_rows, 16), part_rows)
        done = (acc[at, :] + mm(swap, recv_d[at, :])).astype(BF16)
        out_ref[pl.ds(i * (part_rows // CAP), part_rows // CAP)] = done.reshape(part_rows // CAP, CAP, cells)
        return carry

    lax.fori_loop(0, total // part_rows, finish, 0)

    for step in z_order:
        z_copy(step).wait_send()
        c_copy(step).wait_send()
    post(*set_a, lambda copy: copy.wait_send())
    post(*set_d, lambda copy: copy.wait_send())


def run(wn, zn, listed, amps, ints, hole, codes, owner):
    cells = amps.shape[1]
    share = ints.shape[0]
    ki = share * zn
    pairs = hole.shape[0] // wn
    total = wn * CAP * pairs
    blocks = cells // 128
    vmem = pl.BlockSpec(memory_space=pltpu.VMEM)
    dma = pltpu.SemaphoreType.DMA
    return pl.pallas_call(
        functools.partial(kernel, wn, zn),
        out_shape=jax.ShapeDtypeStruct((wn * pairs, CAP, cells), BF16),
        in_specs=[vmem] * 6,
        out_specs=vmem,
        scratch_shapes=[
            pltpu.VMEM((share * 32, 128), BF16),
            pltpu.VMEM((share * 32, 128), F32),
            pltpu.VMEM((ki * 32, 128), BF16),
            pltpu.VMEM((ki + 1, TILE, 128), BF16),
            pltpu.VMEM((NVT * TILE, NVT * TILE), BF16),
            pltpu.VMEM((pairs * blocks * 2 * NVT, NVT * TILE), BF16),
            pltpu.VMEM((pairs, NVT * NVT // 2, 2 * cells), BF16),
            pltpu.VMEM(amps.shape, BF16),
            pltpu.VMEM((total, amps.shape[0]), BF16),
        ] + [pltpu.VMEM((total, cells), BF16)] * 4 + [
            pltpu.VMEM((total, total), BF16),
            pltpu.VMEM((total, cells), F32),
            pltpu.VMEM((1, NVT * NVT), I32),
            pltpu.SMEM((1, NVT * NVT), I32),
            dma,
        ] + [dma((zn,))] * 4 + [dma((wn,))] * 4,
        compiler_params=pltpu.CompilerParams(
            collective_id=0, has_side_effects=True, vmem_limit_bytes=58 * 1024 * 1024
        ),
        cost_estimate=pl.CostEstimate(flops=8 * 10**9, bytes_accessed=4 * 10**6, transcendentals=0),
    )(listed, amps, ints, hole, codes, owner)


def per_device(wn, zn, amplitudes, int_values, hole_ladder, amp_tiles, int_tiles, owner):
    pairs, kt, cells = amplitudes.shape
    ki = int_values.shape[0] * zn
    return run(
        wn,
        zn,
        int_tiles.reshape(1, ki),
        amplitudes.reshape(pairs * kt, cells),
        int_values,
        hole_ladder,
        amp_tiles.reshape(1, kt),
        owner.reshape(1, kt),
    )


def solution(mesh):
    wn, zn = mesh.shape["wide"], mesh.shape["narrow"]
    return jax.shard_map(
        functools.partial(per_device, wn, zn),
        mesh=mesh,
        in_specs=(P("wide", None, "narrow"), P("narrow", None), P(), P(), P(), P()),
        out_specs=P(None, "wide", "narrow"),
        check_vma=False,
    )
```

```python
import functools

import jax
import jax.numpy as jnp
from jax import lax
from jax.experimental import pallas as pl
from jax.experimental.pallas import tpu as pltpu
from jax.sharding import PartitionSpec as P

TILE = 64
NVT = 24
CAP = 4
MESH = pl.DeviceIdType.MESH
NT = (((1,), (1,)), ((), ()))
BF16, F32, I32 = jnp.bfloat16, jnp.float32, jnp.int32


def iota(shape, dim):
    return lax.broadcasted_iota(I32, shape, dim)


def hot(mask):
    return jnp.where(mask, 1.0, 0.0).astype(BF16)


def mm(a, b):
    return jnp.dot(a, b, preferred_element_type=F32)


def column_of(row):
    n = row.shape[1]
    eye = iota((n, n), 0) == iota((n, n), 1)
    return jnp.sum(jnp.where(eye, row, 0), axis=1, keepdims=True)


def near_first(n):
    return sorted(range(1, n), key=lambda d: (min(d, n - d), d))


def kernel(wn, zn, listed_ref, amp_ref, int_ref, hole_ref, codes_ref, owner_ref, out_ref,
           local, local32, gath, tiles, idense, adense, zbuf, dress, pick, send_a, send_d, recv_a, recv_d, hexp, acc,
           table_vec, table_ref, table_sem, z_send, z_recv, c_send, c_recv, a_send, a_recv, d_send, d_recv):
    wide = lax.axis_index("wide")
    narrow = lax.axis_index("narrow")
    core = lax.rem(wide, 2)
    other = wide + 1 - 2 * core
    cells = amp_ref.shape[1]
    blocks = cells // 128
    pairs = hole_ref.shape[0] // wn
    kt = amp_ref.shape[0] // pairs
    rows = CAP * pairs
    total = wn * rows
    part_rows = 8 * rows if wn % 8 == 0 else total
    ki = tiles.shape[0] - 1
    share = ki // zn
    half_rows = share * 16
    cells_all = NVT * NVT
    hf = cells_all // 2
    low = iota((1, 128), 1) < TILE
    z_order = near_first(zn)
    relays = {d: (2 if d == 3 else zn - 2) for d in z_order if min(d, zn - d) == 3}

    def at_z(step):
        return (wide, lax.rem(narrow + step, zn))

    barrier = pltpu.get_barrier_semaphore()
    peers = [d for d in z_order if d not in relays]
    for step in peers:
        pl.semaphore_signal(barrier, inc=1, device_id=at_z(step), device_id_type=MESH)

    def greet(i, c):
        pl.semaphore_signal(barrier, inc=1, device_id=(lax.rem(wide + i, wn), narrow), device_id_type=MESH)
        return c

    lax.fori_loop(1, wn, greet, 0)

    own = int_ref[...].astype(F32)
    for m in range(32):
        local32[pl.ds(m, share, stride=32), :] = own[:, m * 128:(m + 1) * 128]
    local[...] = local32[...].astype(BF16)

    owner_row = owner_ref[...]
    owner_col = column_of(owner_row)
    before = iota((kt, kt), 0) < iota((kt, kt), 1)
    count = jnp.sum(jnp.where(before & (owner_col == owner_row), 1, 0), axis=0, keepdims=True)
    slot = (owner_row * CAP + count) * pairs
    slot = jnp.concatenate([slot + p for p in range(pairs)], axis=1)
    pick[...] = hot(iota((total, pairs * kt), 0) == slot)

    pl.semaphore_wait(barrier, len(peers) + wn - 1)

    def half(shard, who):
        return pl.ds(pl.multiple_of(shard * share * 32 + who * half_rows, 16), half_rows)

    def from_z(step):
        return lax.rem(narrow + zn - step, zn)

    def z_copy(step):
        if step in relays:
            src, to = gath.at[half(from_z(relays[step]), core)], at_z(step - relays[step] + zn)
            dst = gath.at[half(from_z(relays[step]), core)]
        else:
            src, to = local.at[pl.ds(pl.multiple_of(core * half_rows, 16), half_rows)], at_z(step)
            dst = gath.at[half(narrow, core)]
        return pltpu.make_async_remote_copy(
            src_ref=src, dst_ref=dst, send_sem=z_send.at[step], recv_sem=z_recv.at[step], device_id=to,
            device_id_type=MESH)

    def c_copy(step):
        at = gath.at[half(from_z(step), core)]
        return pltpu.make_async_remote_copy(
            src_ref=at, dst_ref=at, send_sem=c_send.at[step], recv_sem=c_recv.at[step], device_id=(other, narrow),
            device_id_type=MESH)

    def spread(block, first):
        n = block.shape[0] // 32
        turned = pltpu.roll(block, TILE, 1)
        tiles[pl.ds(first, n), pl.ds(0, 32)] = jnp.where(low, block, turned).reshape(n, 32, 128)
        tiles[pl.ds(first, n), pl.ds(32, 32)] = jnp.where(low, turned, block).reshape(n, 32, 128)

    def spread_half(step, who):
        spread(gath[half(from_z(step), who), :], from_z(step) * share + who * (share // 2))

    def post(send, recv, s_sem, r_sem, do):
        def one(i, c):
            i = lax.rem(i + 3 * wn // 8, wn - 1) + 1
            to = lax.rem(wide + i, wn)
            do(pltpu.make_async_remote_copy(
                src_ref=send.at[pl.ds(pl.multiple_of(to * rows, 16), rows)],
                dst_ref=recv.at[pl.ds(pl.multiple_of(wide * rows, 16), rows)],
                send_sem=s_sem.at[i], recv_sem=r_sem.at[i], device_id=(to, narrow), device_id_type=MESH))
            return c
        lax.fori_loop(0, wn - 1, one, 0)

    set_a = (send_a, recv_a, a_send, a_recv)
    set_d = (send_d, recv_d, d_send, d_recv)
    mine = pl.ds(pl.multiple_of(wide * rows, 16), rows)

    twos = [d for d in peers if d in relays.values()]
    for step in twos:
        z_copy(step).start()
    send_a[...] = mm(pick[...], amp_ref[...]).astype(BF16)
    post(*set_a, lambda copy: copy.start())
    for step in peers:
        if step not in twos:
            z_copy(step).start()
    recv_a[mine] = send_a[mine]

    spread(local[...], narrow * share)
    tiles[ki] = jnp.zeros((TILE, 128), BF16)

    codes = codes_ref[...]
    second = lax.rem(codes, NVT)
    odd = lax.rem(second, 2)
    cell = lax.div(second, 2) * NVT + lax.div(codes, NVT)
    match = iota((hf, kt), 0) == cell
    onto = jnp.concatenate([hot(match & (odd == 0)), hot(match & (odd == 1))], axis=1)
    lows = jnp.concatenate([low] * blocks, axis=1)
    zero = jnp.zeros((kt, cells), BF16)

    def dense_pair(p):
        a = amp_ref[pl.ds(p * kt, kt), :]
        turned = jnp.concatenate([pltpu.roll(a[:, m * 128:(m + 1) * 128], TILE, 1) for m in range(blocks)], axis=1)
        g0 = mm(onto, jnp.concatenate([jnp.where(lows, a, zero), jnp.where(lows, zero, turned)], axis=0))
        g1 = mm(onto, jnp.concatenate([jnp.where(lows, turned, zero), jnp.where(lows, zero, a)], axis=0))
        for m in range(blocks):
            for h in range(NVT // 2):
                both = jnp.concatenate([v[h * NVT:(h + 1) * NVT, m * 128:(m + 1) * 128] for v in (g0, g1)], axis=0)
                adense[pl.ds((p * blocks + m) * 2 * NVT, 2 * NVT), pl.ds(h * 128, 128)] = both.astype(BF16)

    found = column_of(listed_ref[...]) == iota((ki, cells_all), 1)
    last = jnp.max(jnp.where(found, iota((ki, cells_all), 0), -1), axis=0, keepdims=True)
    table_vec[...] = jnp.where(last < 0, ki, last)
    to_scalar = pltpu.make_async_copy(table_vec, table_ref, table_sem)
    to_scalar.start()
    for p in range(pairs):
        dense_pair(p)
    to_scalar.wait()
    for step in twos:
        z_copy(step).wait_recv()
        for d in relays:
            if relays[d] == step:
                z_copy(d).start()
        c_copy(step).start()
    for step in z_order:
        if step not in twos:
            z_copy(step).wait_recv()
            c_copy(step).start()
            spread_half(step, core)
    for step in twos:
        spread_half(step, core)
    for step in z_order:
        c_copy(step).wait_recv()
        spread_half(step, 1 - core)

    def gather_rows(n):
        for c in range(4):
            for h in range(NVT // 2):
                l = tiles[table_ref[0, (n * 4 + c) * NVT + 2 * h]]
                r = tiles[table_ref[0, (n * 4 + c) * NVT + 2 * h + 1]]
                idense[pl.ds(pl.multiple_of(n * 256 + c * TILE, TILE), TILE), pl.ds(h * 128, 128)] = jnp.where(
                    low, l, r)

    gather_rows(0)

    def product(n, carry):
        rhs = idense[pl.ds(pl.multiple_of(n * 256, 256), 256), :]
        d = lax.dot_general(adense[...], rhs, NT, preferred_element_type=F32)
        gather_rows(lax.rem(n + 1, NVT // 4))
        for p in range(pairs):
            for a in range(2 * blocks):
                x = d[(p * 2 * blocks + a) * NVT:(p * 2 * blocks + a + 1) * NVT]
                both = jnp.concatenate([x[:, :128], x[:, 128:]], axis=0).astype(BF16)
                zbuf[p, pl.ds(pl.multiple_of(n * 2 * NVT, 16), 2 * NVT), pl.ds(a * 128, 128)] = both
        return carry

    lax.fori_loop(0, NVT // 4, product, 0)

    cell_col, odd_col = column_of(cell), column_of(odd)
    match = iota((kt, hf), 1) == cell_col
    take = jnp.concatenate([hot(match & (odd_col == 0)), hot(match & (odd_col == 1))], axis=0)
    u, v = iota((512, 128), 0), iota((512, 128), 1)
    goal = ((u >> 7) & 1) * TILE + (u & 31) * 2 + ((u >> 5) & 1)
    back = hot((v == goal) & (((u >> 8) & 1) == ((u >> 6) & 1)))
    for p in range(pairs):
        got = mm(take, zbuf[p]).astype(BF16)
        for m in range(blocks):
            part_m = got[:, m * 256:(m + 1) * 256]
            flat = jnp.concatenate([part_m[:kt], part_m[kt:]], axis=1)
            dress[pl.ds(p * kt, kt), pl.ds(m * 128, 128)] = mm(flat, back).astype(BF16)
    send_d[...] = mm(pick[...], dress[...]).astype(BF16)
    post(*set_d, lambda copy: copy.start())
    recv_d[mine] = send_d[mine]

    np_all = hole_ref.shape[0]
    r0, c0 = iota((total, np_all), 0), iota((total, np_all), 1)
    by_row = mm(hot(lax.div(r0, CAP) == c0), hole_ref[...]).astype(BF16)
    r1, c1 = iota((np_all, total), 0), iota((np_all, total), 1)
    by_col = hot(lax.div(c1, rows) * pairs + lax.rem(c1, pairs) == r1)
    r2, c2 = iota((part_rows, total), 0), iota((part_rows, total), 1)
    same = lax.rem(r2, CAP) == lax.rem(lax.div(c2, pairs), CAP)
    for i in range(total // part_rows):
        hexp[pl.ds(i * part_rows, part_rows), :] = jnp.where(
            same, mm(by_row[i * part_rows:(i + 1) * part_rows], by_col), 0.0).astype(BF16)
    post(*set_a, lambda copy: copy.wait_recv())

    def ladder(i, carry):
        at = pl.ds(pl.multiple_of(i * part_rows, 16), part_rows)
        acc[at, :] = mm(hexp[at, :], recv_a[...])
        return carry

    lax.fori_loop(0, total // part_rows, ladder, 0)

    r3, c3 = iota((part_rows, part_rows), 0), iota((part_rows, part_rows), 1)
    source = lax.div(r3, rows) * rows + lax.rem(r3, CAP) * pairs + lax.rem(lax.div(r3, CAP), pairs)
    swap = hot(c3 == source)

    post(*set_d, lambda copy: copy.wait_recv())

    def finish(i, carry):
        at = pl.ds(pl.multiple_of(i * part_rows, 16), part_rows)
        done = (acc[at, :] + mm(swap, recv_d[at, :])).astype(BF16)
        out_ref[pl.ds(i * (part_rows // CAP), part_rows // CAP)] = done.reshape(part_rows // CAP, CAP, cells)
        return carry

    lax.fori_loop(0, total // part_rows, finish, 0)

    for step in z_order:
        z_copy(step).wait_send()
        c_copy(step).wait_send()
    post(*set_a, lambda copy: copy.wait_send())
    post(*set_d, lambda copy: copy.wait_send())


def run(wn, zn, listed, amps, ints, hole, codes, owner):
    cells = amps.shape[1]
    share = ints.shape[0]
    ki = share * zn
    pairs = hole.shape[0] // wn
    total = wn * CAP * pairs
    blocks = cells // 128
    vmem = pl.BlockSpec(memory_space=pltpu.VMEM)
    dma = pltpu.SemaphoreType.DMA
    return pl.pallas_call(
        functools.partial(kernel, wn, zn),
        out_shape=jax.ShapeDtypeStruct((wn * pairs, CAP, cells), BF16),
        in_specs=[vmem] * 6,
        out_specs=vmem,
        scratch_shapes=[
            pltpu.VMEM((share * 32, 128), BF16),
            pltpu.VMEM((share * 32, 128), F32),
            pltpu.VMEM((ki * 32, 128), BF16),
            pltpu.VMEM((ki + 1, TILE, 128), BF16),
            pltpu.VMEM((NVT * TILE, NVT * TILE), BF16),
            pltpu.VMEM((pairs * blocks * 2 * NVT, NVT * TILE), BF16),
            pltpu.VMEM((pairs, NVT * NVT // 2, 2 * cells), BF16),
            pltpu.VMEM(amps.shape, BF16),
            pltpu.VMEM((total, amps.shape[0]), BF16),
        ] + [pltpu.VMEM((total, cells), BF16)] * 4 + [
            pltpu.VMEM((total, total), BF16),
            pltpu.VMEM((total, cells), F32),
            pltpu.VMEM((1, NVT * NVT), I32),
            pltpu.SMEM((1, NVT * NVT), I32),
            dma,
        ] + [dma((zn,))] * 4 + [dma((wn,))] * 4,
        compiler_params=pltpu.CompilerParams(
            collective_id=0, has_side_effects=True, vmem_limit_bytes=40 * 1024 * 1024
        ),
        cost_estimate=pl.CostEstimate(flops=8 * 10**9, bytes_accessed=4 * 10**6, transcendentals=0),
    )(listed, amps, ints, hole, codes, owner)


def per_device(wn, zn, amplitudes, int_values, hole_ladder, amp_tiles, int_tiles, owner):
    pairs, kt, cells = amplitudes.shape
    ki = int_values.shape[0] * zn
    return run(
        wn,
        zn,
        int_tiles.reshape(1, ki),
        amplitudes.reshape(pairs * kt, cells),
        int_values,
        hole_ladder,
        amp_tiles.reshape(1, kt),
        owner.reshape(1, kt),
    )


def solution(mesh):
    wn, zn = mesh.shape["wide"], mesh.shape["narrow"]
    return jax.shard_map(
        functools.partial(per_device, wn, zn),
        mesh=mesh,
        in_specs=(P("wide", None, "narrow"), P("narrow", None), P(), P(), P(), P()),
        out_specs=P(None, "wide", "narrow"),
        check_vma=False,
    )
```
